512 devices in a mesh: lon: 32 (over z_lo, y, core), ch: 16 (over x, z_hi).
Axes of the slice: x: 4, y: 8, z: 8 (z_hi: 4, z_lo: 2; z = z_hi * 2 + z_lo), core: 2. Of those that a mesh axis runs over, the one named last changes fastest.
Arguments:
- grid_state: bfloat16 [128, 512, 1024], P(None, 'lon', 'ch'), may hold values from -40 to 40
- first_gain: bfloat16 [1024], P('ch'), may hold values from 0.099609375 to 1.8984375
- spectral_first: bfloat16 [2, 1024, 64], P(None, 'ch'), may hold values from -0.5 to 0.5
- spectral_second: bfloat16 [2, 1024, 64], P(None, 'ch'), may hold values from -0.5 to 0.5
- second_gain: bfloat16 [1024], P('ch'), may hold values from 0.099609375 to 1.8984375
- up_weight: bfloat16 [1024, 4096], P(None, 'ch'), may hold values from -0.1875 to 0.1875
- down_weight: bfloat16 [4096, 1024], P('ch'), may hold values from -0.125 to 0.125
Outputs:
- block_out: bfloat16 [128, 512, 1024], P(None, 'lon', 'ch')
The draws below stay inside these ranges and needn't reach their ends.
All inputs are finite; a program needn't handle non-finite values.
Results may differ from the reference program's by a relative error of at most 0.015.
Values may be sent and summed in bfloat16 or wider, within the bound.
No kernel may reach another device: no remote copies, remote signals or barrier semaphores. Data moves between devices by JAX's collectives and lax.ppermute only.
A program may use at most 64 MiB of HBM per device.

```python
import math
import jax
import jax.numpy as jnp
from jax import lax

H = 128
W = 512
C = 1024
BLOCK = 64
KW = 256
HID = 4096
N_CH = 16


def draw_grid_state(key, part):
    key_base, key_rows = jax.random.split(key, 2)
    channel_scale = 0.3 * jnp.exp(jnp.log(10.0) * jnp.arange(C, dtype=jnp.float32) / (C - 1))
    row_log = jax.random.uniform(key_rows, (H, W, 1), jnp.float32, jnp.log(0.3), jnp.log(3.0))
    base = jnp.clip(jax.random.normal(key_base, (H, W, C), jnp.float32), -3.0, 3.0)
    values = base * channel_scale * jnp.exp(row_log)
    return values.astype(jnp.bfloat16)


def with_spikes(drawn, own_key, source, target, shards_of, factor):
    owner, partner = [(jnp.arange(drawn.shape[position]) // (drawn.shape[position] // shards_of)).reshape([-1 if axis == position else 1 for axis in range(drawn.ndim)]) for position in (source, target)]
    chosen = jax.random.permutation(own_key, shards_of)[partner]
    strong = (owner == chosen) | (owner == (partner + shards_of // 2) % shards_of)
    return jnp.where(strong, factor * drawn, drawn)


def shard_levels(stream_key, extent, cuts, least, largest):
    level, own = 1.0, jax.random.fold_in(stream_key, 6)
    for position, blocks in cuts:
        draws = jnp.exp(jax.random.uniform(jax.random.fold_in(own, position), (blocks,), jnp.float32, least / len(cuts), largest / len(cuts)))
        level = level * jnp.repeat(draws, extent[position] // blocks).reshape([-1 if axis == position else 1 for axis in range(len(extent))])
    return level


def gaussian(stream_key, shape, scale, bound, cuts=(), kind=jnp.bfloat16):
    array = jax.random.normal(stream_key, shape, jnp.float32) * scale
    if len(cuts) > 0:
        array = shard_levels(stream_key, shape, cuts, -0.22, 0.18) * array
    return jnp.clip(array, min=-bound, max=bound).astype(kind)


def bell_draw_with(stream_key, shape, scale, bound, cuts, heavy, held_as=jnp.bfloat16):
    drawn = scale * jax.random.normal(stream_key, shape, jnp.float32)
    if cuts:
        drawn = drawn * shard_levels(stream_key, shape, cuts, -0.22, 0.18)
    return jnp.clip(with_spikes(drawn, jax.random.fold_in(stream_key, 3), *heavy), -bound, bound).astype(held_as)


def setup_inputs(seed: int = 0) -> dict:
    arg_keys = jax.random.split(jax.random.key(seed), 8)
    grid_state = draw_grid_state(jax.random.fold_in(arg_keys[7], 71), 0)
    first_gain = jnp.clip(1.0 + 0.18 * jax.random.normal(arg_keys[1], (C,), jnp.float32), 0.099609375, 1.8984375).astype(jnp.bfloat16)
    spectral_first = gaussian(arg_keys[2], (2, C, BLOCK), (2 * BLOCK) ** -0.5, 0.5, ((1, 16),))
    spectral_second = gaussian(arg_keys[3], (2, C, BLOCK), (2 * BLOCK) ** -0.5, 0.5, ((1, 16),))
    second_gain = jnp.clip(1.0 + 0.18 * jax.random.normal(arg_keys[4], (C,), jnp.float32), 0.099609375, 1.8984375).astype(jnp.bfloat16)
    up_weight = gaussian(arg_keys[5], (C, HID), C ** -0.5, 0.1875, ((1, 16),))
    down_weight = bell_draw_with(arg_keys[6], (HID, C), HID ** -0.5, 0.125, ((0, 16),), (0, 1, 16, 2.0))
    return {"grid_state": grid_state, "first_gain": first_gain, "spectral_first": spectral_first, "spectral_second": spectral_second, "second_gain": second_gain, "up_weight": up_weight, "down_weight": down_weight}


EPSILON = 1e-05
THRESHOLD = 0.1
HIGHEST = lax.Precision.HIGHEST

def normalize(values, total, square, gain, width):
    centre = total[..., None] / width
    spread = square[..., None] / width - centre * centre
    return ((values - centre) * lax.rsqrt(spread + EPSILON) * gain).astype(jnp.bfloat16)

def soft_shrink(values):
    return values - jnp.clip(values, -THRESHOLD, THRESHOLD)

def to_half(values):
    return lax.optimization_barrier(values.astype(jnp.bfloat16)).astype(jnp.float32)

def complex_mix(real_part, imag_part, weight):
    lat_len, mode_len, width_all = real_part.shape
    block_width = weight.shape[-1]
    blocks = width_all // block_width
    w_real = weight[0].astype(jnp.float32).reshape(blocks, block_width, block_width)
    w_imag = weight[1].astype(jnp.float32).reshape(blocks, block_width, block_width)
    real_blocks = real_part.reshape(lat_len, mode_len, blocks, block_width)
    imag_blocks = imag_part.reshape(lat_len, mode_len, blocks, block_width)

    def product(left, right):
        return jnp.einsum('hknb,nbd->hknd', left, right, precision=HIGHEST)
    new_real = product(real_blocks, w_real) - product(imag_blocks, w_imag)
    new_imag = product(real_blocks, w_imag) + product(imag_blocks, w_real)
    return (new_real.reshape(lat_len, mode_len, width_all), new_imag.reshape(lat_len, mode_len, width_all))

def reference(grid_state, first_gain, spectral_first, spectral_second, second_gain, up_weight, down_weight):
    values = grid_state.astype(jnp.float32)
    normed_first = normalize(values, lax.optimization_barrier(jnp.sum(values, axis=2)), lax.optimization_barrier(jnp.sum(values * values, axis=2)), first_gain, C)
    spectrum = jnp.fft.rfft2(normed_first.astype(jnp.float32), axes=(0, 1), norm='ortho')[:, :KW, :]
    spec_real = to_half(jnp.real(spectrum))
    spec_imag = to_half(jnp.imag(spectrum))
    mid_real, mid_imag = complex_mix(spec_real, spec_imag, spectral_first)
    mid_real = to_half(jax.nn.relu(mid_real))
    mid_imag = to_half(jax.nn.relu(mid_imag))
    out_real, out_imag = complex_mix(mid_real, mid_imag, spectral_second)
    out_real = soft_shrink(out_real)
    out_imag = soft_shrink(out_imag)
    shrunk = lax.complex(out_real, out_imag)
    shrunk = jnp.pad(shrunk, ((0, 0), (0, W // 2 + 1 - KW), (0, 0)))
    filtered = jnp.fft.irfft2(shrunk, s=(H, W), axes=(0, 1), norm='ortho').astype(jnp.bfloat16)
    mixed = (values + normed_first.astype(jnp.float32) + filtered.astype(jnp.float32)).astype(jnp.bfloat16)
    wide = mixed.astype(jnp.float32)
    normed_second = normalize(wide, lax.optimization_barrier(jnp.sum(wide, axis=2)), lax.optimization_barrier(jnp.sum(wide * wide, axis=2)), second_gain, C)
    shard_width = HID // N_CH
    block_rows = math.gcd(H * W, 4096)
    down_split = down_weight.astype(jnp.float32).reshape(N_CH, shard_width, C)

    def block_mlp(token_block):
        upward = jnp.dot(token_block, up_weight, preferred_element_type=jnp.float32)
        hidden = jax.nn.gelu(upward).astype(jnp.bfloat16)
        pieces = hidden.astype(jnp.float32).reshape(block_rows, N_CH, shard_width)
        partial_sum = jnp.einsum('tsj,sjc->tsc', pieces, down_split)
        rounded = lax.optimization_barrier(partial_sum.astype(jnp.bfloat16))
        return lax.optimization_barrier(jnp.sum(rounded.astype(jnp.float32), axis=1))
    branch = lax.map(block_mlp, normed_second.reshape(H * W // block_rows, block_rows, C))
    return (wide + branch.reshape(H, W, C)).astype(jnp.bfloat16)
```

```python
import math

import jax
import jax.numpy as jnp
import numpy as np
from jax import lax
from jax.sharding import Mesh
from jax.sharding import PartitionSpec as P

EPSILON = 1e-05
THRESHOLD = 0.1
LAT = 128
LON = 512
KW = 256
C = 1024
F32 = jnp.float32
BF16 = jnp.bfloat16

LON_AXES = ("zl", "y", "core")
QUAD = ("zl", "core")


def lat_table():
    lat = np.arange(LAT)
    rows = np.zeros((LAT, LAT))
    for mode in range(LAT // 2):
        phase = 2.0 * math.pi * ((lat * mode) % LAT) / LAT
        rows[2 * mode] = np.cos(phase)
        rows[2 * mode + 1] = np.sin(phase)
    rows[1] = np.cos(math.pi * lat)
    return rows / math.sqrt(LAT)


def lon_table():
    phase = 2.0 * math.pi * ((np.arange(KW)[:, None] * np.arange(LON)[None, :]) % LON) / LON
    return np.concatenate([np.cos(phase), np.sin(phase)]) / math.sqrt(LON)


def lon_inverse_table():
    weight = np.where(np.arange(KW) == 0, 1.0, 2.0)
    return lon_table().T * np.concatenate([weight, weight])[None, :]


def shrink(values):
    return values - jnp.clip(values, -THRESHOLD, THRESHOLD)


def mix_tables(first, second, special):
    wr, wi = first[0], first[1]
    zero = jnp.zeros_like(wr)
    plain = jnp.concatenate(
        [
            jnp.concatenate([wr, wi, wr, wi], axis=1),
            jnp.concatenate([wi, -wr, -wi, wr], axis=1),
            jnp.concatenate([wi, -wr, wi, -wr], axis=1),
            jnp.concatenate([-wr, -wi, wr, wi], axis=1),
        ]
    )
    edge = jnp.concatenate(
        [
            jnp.concatenate([wr, wi, zero, zero], axis=1),
            jnp.concatenate([zero, zero, wr, wi], axis=1),
            jnp.concatenate([wi, -wr, zero, zero], axis=1),
            jnp.concatenate([zero, zero, wi, -wr], axis=1),
        ]
    )
    vr, vi = second[0], second[1]
    none = jnp.zeros((128, 64), vr.dtype)
    real = jnp.concatenate([vr, -vi])
    imag = jnp.concatenate([vi, vr])

    def columns(pieces):
        return jnp.concatenate(
            [jnp.concatenate([top, bottom]) for top, bottom in pieces], axis=1
        )

    plain_out = columns(
        [
            (real, none),
            (-imag, none),
            (none, real),
            (none, imag),
            (-imag, none),
            (-real, none),
            (none, -imag),
            (none, real),
        ]
    )
    edge_out = columns(
        [
            (real, none),
            (none, real),
            (none, none),
            (none, none),
            (-imag, none),
            (none, -imag),
            (none, none),
            (none, none),
        ]
    )
    mix_in = jnp.stack([jnp.where(special, edge, plain), plain])
    mix_out = jnp.stack([jnp.where(special, edge_out, plain_out), plain_out])
    return mix_in, mix_out


def per_device(grid_state, first_gain, spectral_first, spectral_second, second_gain, up_weight, down_weight):
    quarter = lax.axis_index("zl") * 2 + lax.axis_index("core")
    special = (lax.axis_index("zl") + lax.axis_index("y") + lax.axis_index("core")) == 0
    part = up_weight.shape[1] // 4
    up_part = lax.dynamic_slice_in_dim(up_weight, quarter * part, part, axis=1).T
    down_part = lax.dynamic_slice_in_dim(down_weight, quarter * part, part, axis=0)
    weights = lax.all_gather(jnp.stack([up_part, down_part]), "ch", axis=0)

    tokens = grid_state.transpose(1, 2, 0)
    values = tokens.astype(F32)
    gain_row = jnp.pad(second_gain.astype(F32), (0, 64))[None]
    sums = jnp.concatenate([jnp.sum(values, axis=1), jnp.sum(values * values, axis=1), gain_row])
    sums = jnp.pad(sums, ((0, 7), (0, 0)))
    sums = lax.all_to_all(jnp.broadcast_to(sums[None], (16, 40, 128)), "ch", 0, 0)
    second_all = sums[:, 32, :64].reshape(C, 1)
    sums = jnp.sum(sums[:, :32], axis=0)
    centre = sums[:16] / C
    spread = sums[16:] / C - centre * centre
    scale = lax.rsqrt(spread + EPSILON)
    normed = (
        (values - centre[:, None]) * scale[:, None] * first_gain.astype(F32)[None, :, None]
    ).astype(BF16)

    table = jnp.asarray(lat_table().reshape(32, 4, LAT), BF16)
    rows = jnp.einsum("lqh,wch->lwqc", table, normed, preferred_element_type=F32)
    rows = rows.astype(BF16).reshape(32, 16, 256)
    rows = lax.all_to_all(rows, LON_AXES, 0, 0).reshape(LON, 256)

    waves = jnp.dot(jnp.asarray(lon_table(), BF16), rows, preferred_element_type=F32).astype(BF16)
    mix_in, mix_out = mix_tables(spectral_first, spectral_second, special)
    outs = []
    for pair in range(2):
        lanes = slice(pair * 128, pair * 128 + 128)
        middle = jnp.dot(waves[:KW, lanes], mix_in[pair, :128], preferred_element_type=F32)
        middle += jnp.dot(waves[KW:, lanes], mix_in[pair, 128:], preferred_element_type=F32)
        middle = jax.nn.relu(middle).astype(BF16)
        mixed_modes = shrink(jnp.dot(middle, mix_out[pair], preferred_element_type=F32))
        outs.append(
            jnp.concatenate(
                [
                    mixed_modes[:, :128] + mixed_modes[:, 128:256],
                    mixed_modes[:, 256:384] + mixed_modes[:, 384:],
                ]
            ).astype(BF16)
        )
    modes = jnp.concatenate(outs, axis=1)
    back = jnp.dot(jnp.asarray(lon_inverse_table(), BF16), modes, preferred_element_type=F32)
    back = lax.all_to_all(back.astype(BF16).reshape(32, 16, 256), LON_AXES, 0, 0)
    filtered = jnp.einsum(
        "lqh,lwqc->wch", table, back.reshape(32, 16, 4, 64), preferred_element_type=F32
    ).astype(BF16)
    mixed = (values + normed.astype(F32) + filtered.astype(F32)).astype(BF16)

    wide = lax.all_to_all(mixed, "ch", 0, 0).reshape(C, 128).astype(F32)
    mean = jnp.sum(wide, axis=0, keepdims=True) / C
    power = jnp.sum(wide * wide, axis=0, keepdims=True) / C - mean * mean
    normed_second = ((wide - mean) * lax.rsqrt(power + EPSILON) * second_all).astype(BF16)
    group = lax.all_to_all(jnp.broadcast_to(normed_second[None], (4, C, 128)), QUAD, 0, 0)
    upward = jnp.einsum("sjd,idt->isjt", weights[:, 0], group, preferred_element_type=F32)
    hidden = jax.nn.gelu(upward).astype(BF16)
    sums_out = jnp.einsum("sjc,isjt->ict", weights[:, 1], hidden, preferred_element_type=F32)
    sums_out = lax.all_to_all(sums_out.astype(BF16), QUAD, 0, 0)
    branch = jnp.sum(sums_out.astype(F32), axis=0).astype(BF16).reshape(16, 64, 128)
    branch = lax.all_to_all(branch, "ch", 0, 0)
    return (mixed.astype(F32) + branch.astype(F32)).astype(BF16).transpose(2, 0, 1)


def solution(mesh):
    fine = Mesh(mesh.devices.reshape(2, 8, 2, 16), ("zl", "y", "core", "ch"))
    return jax.shard_map(
        per_device,
        mesh=fine,
        in_specs=(
            P(None, LON_AXES, "ch"),
            P("ch"),
            P(None, "ch", None),
            P(None, "ch", None),
            P("ch"),
            P(None, "ch"),
            P("ch", None),
        ),
        out_specs=P(None, LON_AXES, "ch"),
        check_vma=False,
    )
```

```python
import math

import jax
import jax.numpy as jnp
import numpy as np
from jax import lax
from jax.experimental import pallas as pl
from jax.experimental.pallas import tpu as pltpu
from jax.sharding import Mesh
from jax.sharding import PartitionSpec as P

EPSILON = 1e-05
THRESHOLD = 0.1
LAT = 128
GAIN_ROW = 416
LON = 512
KW = 256
C = 1024
F32 = jnp.float32
BF16 = jnp.bfloat16
VMEM = pl.BlockSpec(memory_space=pltpu.VMEM)
PARAMS = pltpu.CompilerParams(vmem_limit_bytes=10 << 20)

LON_AXES = ("zl", "y", "core")
CH_AXES = ("xh", "xl", "zh")
OCT_AXES = ("xl", "zh")
NT = (((1,), (1,)), ((), ()))
TN = (((0,), (0,)), ((), ()))


def lat_table():
    lat = np.arange(LAT)
    rows = np.zeros((LAT, LAT))
    for mode in range(LAT // 2):
        phase = 2.0 * math.pi * ((lat * mode) % LAT) / LAT
        rows[2 * mode] = np.cos(phase)
        rows[2 * mode + 1] = np.sin(phase)
    rows[1] = np.cos(math.pi * lat)
    return rows / math.sqrt(LAT)


def lat_pairs():
    table = lat_table().reshape(32, 2, 2, LAT)
    return table.transpose(1, 0, 2, 3).reshape(64, 2 * LAT)


def lon_table():
    phase = 2.0 * math.pi * ((np.arange(KW)[:, None] * np.arange(LON)[None, :]) % LON) / LON
    return np.concatenate([np.cos(phase), np.sin(phase)]) / math.sqrt(LON)


def lon_inverse_table():
    weight = np.where(np.arange(KW) == 0, 1.0, 2.0)
    return lon_table().T * np.concatenate([weight, weight])[None, :]


SIGNS_IN = np.array(
    [
        [[1, 0, 1, 0], [0, -1, 0, 1], [0, -1, 0, -1], [-1, 0, 1, 0]],
        [[0, 1, 0, 1], [1, 0, -1, 0], [1, 0, 1, 0], [0, -1, 0, 1]],
        [[1, 0, 0, 0], [0, 0, 1, 0], [0, -1, 0, 0], [0, 0, 0, -1]],
        [[0, 1, 0, 0], [0, 0, 0, 1], [1, 0, 0, 0], [0, 0, 1, 0]],
    ]
)
SIGNS_OUT = np.array(
    [
        [
            [1, 0, 0, 0, 0, -1, 0, 0],
            [0, -1, 0, 0, -1, 0, 0, 0],
            [0, 0, 1, 0, 0, 0, 0, 1],
            [0, 0, 0, 1, 0, 0, -1, 0],
        ],
        [
            [0, -1, 0, 0, -1, 0, 0, 0],
            [-1, 0, 0, 0, 0, 1, 0, 0],
            [0, 0, 0, 1, 0, 0, -1, 0],
            [0, 0, -1, 0, 0, 0, 0, -1],
        ],
        [
            [1, 0, 0, 0, 0, 0, 0, 0],
            [0, 0, 0, 0, -1, 0, 0, 0],
            [0, 1, 0, 0, 0, 0, 0, 0],
            [0, 0, 0, 0, 0, -1, 0, 0],
        ],
        [
            [0, 0, 0, 0, -1, 0, 0, 0],
            [-1, 0, 0, 0, 0, 0, 0, 0],
            [0, 0, 0, 0, 0, -1, 0, 0],
            [0, -1, 0, 0, 0, 0, 0, 0],
        ],
    ]
)


def sign_rows(signs):
    wide = np.repeat(signs, 64, axis=2)
    return np.pad(wide, ((0, 0), (0, 4), (0, 0)))


def shrink(values):
    return values - jnp.clip(values, -THRESHOLD, THRESHOLD)


def column_of(row):
    size = row.shape[1]
    diagonal = lax.broadcasted_iota(jnp.int32, (size, size), 0) == lax.broadcasted_iota(
        jnp.int32, (size, size), 1
    )
    return jnp.sum(jnp.where(diagonal, row, 0.0), axis=1, keepdims=True)


def setup_kernel(place_ref, up_ref, down_ref, tokens_ref, gain_ref, packed_ref, sums_ref, up_part, tokens_part, gain_part, sems):
    half = pl.ds(pl.multiple_of(place_ref[0] * 128, 128), 128)
    pairs = [
        (tokens_ref, tokens_part),
        (gain_ref, gain_part),
        (up_ref.at[:, half], up_part),
        (down_ref.at[half], packed_ref.at[1]),
    ]
    copies = [pltpu.make_async_copy(a, b, sems.at[i]) for i, (a, b) in enumerate(pairs)]
    for copy in copies:
        copy.start()
    copies[0].wait()
    copies[1].wait()
    values = tokens_part[...].astype(F32)
    gain = gain_part[...].astype(F32).reshape(1, 64)
    block = jnp.concatenate(
        [
            jnp.sum(values, axis=1),
            jnp.sum(values * values, axis=1),
            jnp.broadcast_to(jnp.concatenate([gain, gain], axis=1), (8, 128)),
        ]
    )
    sums_ref[...] = jnp.broadcast_to(block[None], sums_ref.shape)
    copies[2].wait()
    row = lax.broadcasted_iota(jnp.int32, (128, 128), 0)
    lane = lax.broadcasted_iota(jnp.int32, (128, 128), 1)
    pick = jnp.where(lane == row, 1.0, 0.0).astype(BF16)
    packed_ref[0] = lax.dot_general(pick, up_part[...], NT, preferred_element_type=F32).astype(BF16)
    copies[3].wait()


def setup(*args):
    return pl.pallas_call(
        setup_kernel,
        out_shape=[shape((2, 128, C)), shape((16, 40, 128), F32)],
        in_specs=[pl.BlockSpec(memory_space=pltpu.SMEM)] + [pl.BlockSpec(memory_space=pl.ANY)] * 4,
        out_specs=[VMEM] * 2,
        scratch_shapes=[
            pltpu.VMEM((C, 128), BF16),
            pltpu.VMEM((16, 64, 128), BF16),
            pltpu.VMEM((64,), BF16),
            pltpu.SemaphoreType.DMA((4,)),
        ],
        compiler_params=pltpu.CompilerParams(vmem_limit_bytes=60 << 20),
        name="setup",
    )(*args)


def forward_kernel(sums_ref, tokens_ref, small_ref, normed_ref, out_ref, twice, wide):
    total = jnp.sum(sums_ref[:, :32, :], axis=0)
    centre = total[:16] / C
    spread = total[16:] / C - centre * centre
    scale = lax.rsqrt(spread + EPSILON)
    gain = column_of(small_ref[GAIN_ROW : GAIN_ROW + 1, :64].astype(F32))
    twice[...] = jnp.zeros_like(twice)
    table = small_ref[:64]
    for w in range(16):
        values = tokens_ref[w].astype(F32)
        normed = ((values - centre[w : w + 1]) * scale[w : w + 1] * gain).astype(BF16)
        normed_ref[w] = normed
        slot = w % 2
        twice[slot, :64, :LAT] = normed
        twice[slot, 64:, LAT:] = normed
        rows = lax.dot_general(table, twice[slot], NT, preferred_element_type=F32)
        wide[:, w, :128] = rows[:32]
        wide[:, w, 128:] = rows[32:]
    out_ref[...] = wide[...].astype(BF16)


def spectral_kernel(place_ref, rows_ref, lon_ref, inverse_ref, small_ref, out_ref, modes):
    waves = jnp.dot(lon_ref[...], rows_ref[...], preferred_element_type=F32).astype(BF16)
    row = lax.broadcasted_iota(jnp.int32, (256, 8), 0) // 64
    spot = lax.broadcasted_iota(jnp.int32, (256, 8), 1)
    blocks = jnp.where(row == spot, 1.0, 0.0).astype(BF16)
    down64 = lax.broadcasted_iota(jnp.int32, (256, 64), 0) % 64
    stack = jnp.where(down64 == lax.broadcasted_iota(jnp.int32, (256, 64), 1), 1.0, 0.0).astype(BF16)

    def tables(weights, signs, columns):
        lane = lax.broadcasted_iota(jnp.int32, (64, columns), 1) % 64
        spread = jnp.where(lane == lax.broadcasted_iota(jnp.int32, (64, columns), 0), 1.0, 0.0)
        spread = spread.astype(BF16)
        tiles = []
        for part in range(2):
            tall = jnp.dot(stack, weights[part], preferred_element_type=F32).astype(BF16)
            tiles.append(jnp.dot(tall, spread, preferred_element_type=F32))
        found = []
        for kind in (0, 2):
            mask = [
                jnp.dot(blocks, signs[kind + part], preferred_element_type=F32)
                for part in range(2)
            ]
            found.append(tiles[0] * mask[0] + tiles[1] * mask[1])
        plain, edge = found
        return [jnp.where(place_ref[1] == 1, edge, plain).astype(BF16), plain.astype(BF16)]

    def rows_of(start, count):
        return small_ref[start : start + count]

    first = [rows_of(160 + 64 * part, 64)[:, :64] for part in range(2)]
    second = [rows_of(288 + 64 * part, 64)[:, :64] for part in range(2)]
    signs_in = [rows_of(64 + 8 * kind, 8) for kind in range(4)]
    signs_out = [
        jnp.concatenate([rows_of(96 + 8 * kind, 8), rows_of(128 + 8 * kind, 8)], axis=1)
        for kind in range(4)
    ]
    mix_in = tables(first, signs_in, 256)
    mix_out = tables(second, signs_out, 512)
    for pair in range(2):
        lanes = slice(pair * 128, pair * 128 + 128)
        middle = jnp.dot(waves[:KW, lanes], mix_in[pair][:128], preferred_element_type=F32)
        middle += jnp.dot(waves[KW:, lanes], mix_in[pair][128:], preferred_element_type=F32)
        middle = jnp.maximum(middle, 0.0).astype(BF16)
        back = shrink(jnp.dot(middle, mix_out[pair], preferred_element_type=F32))
        modes[:KW, lanes] = (back[:, :128] + back[:, 128:256]).astype(BF16)
        modes[KW:, lanes] = (back[:, 256:384] + back[:, 384:]).astype(BF16)
    out_ref[...] = jnp.dot(inverse_ref[...], modes[...], preferred_element_type=F32).astype(BF16)


def inverse_kernel(rows_ref, tokens_ref, normed_ref, small_ref, mixed_ref, wide):
    wide[...] = rows_ref[...].astype(F32)
    table = small_ref[:64]
    for w in range(16):
        rows = jnp.concatenate([wide[:, w, :128], wide[:, w, 128:]]).astype(BF16)
        both = lax.dot_general(rows, table, TN, preferred_element_type=F32)
        filtered = (both[:64, :LAT] + both[64:, LAT:]).astype(BF16).astype(F32)
        mixed = tokens_ref[w].astype(F32) + normed_ref[w].astype(F32) + filtered
        mixed_ref[w] = mixed.astype(BF16)


def second_norm_kernel(place_ref, own_ref, other_ref, sums_ref, out_ref, both):
    xh = place_ref[2]
    for w in range(2):
        for d in range(8):
            mine = pl.ds(pl.multiple_of(xh * 512 + d * 64, 64), 64)
            theirs = pl.ds(pl.multiple_of((1 - xh) * 512 + d * 64, 64), 64)
            both[mine, w * 128 : w * 128 + 128] = own_ref[d, w].astype(F32)
            both[theirs, w * 128 : w * 128 + 128] = other_ref[d, w].astype(F32)
    wide = both[...]
    mean = jnp.sum(wide, axis=0, keepdims=True) / C
    power = jnp.sum(wide * wide, axis=0, keepdims=True) / C - mean * mean
    scale = lax.rsqrt(power + EPSILON)
    for block in range(16):
        rows = slice(block * 64, block * 64 + 64)
        gain = column_of(sums_ref[block, 32:33, :64])
        out_ref[rows] = ((both[rows] - mean) * scale * gain).astype(BF16)


def mlp_kernel(*refs):
    pieces = refs[:8]
    own_ref, other_ref, own_out, other_out = refs[8:]
    group = jnp.concatenate([own_ref[...], other_ref[...]], axis=1)
    total = None
    for first, second in zip(pieces[0::2], pieces[1::2]):
        up = jnp.concatenate([first[0], second[0]])
        down = jnp.concatenate([first[1], second[1]])
        upward = jnp.dot(up, group, preferred_element_type=F32)
        hidden = jax.nn.gelu(upward).astype(BF16)
        found = lax.dot_general(down, hidden, TN, preferred_element_type=F32)
        total = found if total is None else total + found
    own_out[...] = total[:, :256]
    other_out[...] = total[:, 256:].astype(BF16)


def core_sum_kernel(place_ref, own_ref, other_ref, keep_ref, send_ref):
    xh = place_ref[2]
    mine = pl.ds(pl.multiple_of(xh * 512, 512), 512)
    theirs = pl.ds(pl.multiple_of((1 - xh) * 512, 512), 512)
    keep_ref[...] = own_ref[mine] + other_ref[mine].astype(F32)
    send_ref[...] = (own_ref[theirs] + other_ref[theirs].astype(F32)).astype(BF16)


def finish_kernel(mixed_ref, keep_ref, other_ref, out_ref):
    for d in range(8):
        rows = slice(d * 64, d * 64 + 64)
        branch = keep_ref[rows] + other_ref[rows].astype(F32)
        for w in range(2):
            sums = mixed_ref[d, w].astype(F32) + branch[:, w * 128 : w * 128 + 128]
            out_ref[d, w] = sums.astype(BF16)


def call(kernel, shapes, scratch, name, args, scalars=0, limit=10 << 20):
    specs = [pl.BlockSpec(memory_space=pltpu.SMEM)] * scalars + [VMEM] * (len(args) - scalars)
    many = isinstance(shapes, list)
    return pl.pallas_call(
        kernel,
        out_shape=shapes,
        in_specs=specs,
        out_specs=[VMEM] * len(shapes) if many else VMEM,
        scratch_shapes=scratch,
        compiler_params=pltpu.CompilerParams(vmem_limit_bytes=limit),
        name=name,
    )(*args)


def shape(dims, kind=BF16):
    return jax.ShapeDtypeStruct(dims, kind)


def swap(values, axis):
    return lax.ppermute(values, axis, [(0, 1), (1, 0)])


def next_pair(values):
    pairs = []
    for zh in range(4):
        pairs.append((4 + zh, (zh + 1) % 4))
        pairs.append((zh, 4 + (zh - 1) % 4))
    return lax.ppermute(values, ("zl", "zh"), pairs)


def per_device(grid_state, first_gain, spectral_first, spectral_second, second_gain, up_weight, down_weight):
    zl, core = lax.axis_index("zl"), lax.axis_index("core")
    edge = (zl + lax.axis_index("y") + core) == 0
    place = jnp.stack([core, edge.astype(jnp.int32), lax.axis_index("xh")])
    tokens = grid_state.transpose(1, 2, 0)
    packed, sums = setup(place, up_weight, down_weight, tokens, second_gain)
    z0 = next_pair(packed)
    x0 = swap(packed, "xl")
    sums = lax.all_to_all(sums, CH_AXES, 0, 0)
    signs_out = sign_rows(SIGNS_OUT).reshape(32, 512)
    small = jnp.concatenate(
        [
            jnp.asarray(lat_pairs(), BF16),
            jnp.asarray(sign_rows(SIGNS_IN).reshape(32, 256), BF16),
            jnp.asarray(signs_out[:, :256], BF16),
            jnp.asarray(signs_out[:, 256:], BF16),
            jnp.pad(spectral_first.reshape(128, 64), ((0, 0), (0, 192))),
            jnp.pad(spectral_second.reshape(128, 64), ((0, 0), (0, 192))),
            jnp.pad(first_gain[None], ((0, 15), (0, 192))),
        ]
    )
    sums, small, z0, x0 = lax.optimization_barrier((sums, small, z0, x0))
    normed, rows = call(
        forward_kernel,
        [shape((16, 64, 128)), shape((32, 16, 256))],
        [pltpu.VMEM((2, 128, 256), BF16), pltpu.VMEM((32, 16, 256), F32)],
        "norm_latitude",
        (sums, tokens, small),
    )
    rows, z0 = lax.optimization_barrier((rows, z0))
    z1 = swap(z0, "zl")
    x1 = swap(z0, "xl")
    rows = lax.all_to_all(rows, LON_AXES, 0, 0)
    rows, z1, x1 = lax.optimization_barrier((rows, z1, x1))
    back = call(
        spectral_kernel,
        shape((LON, 256)),
        [pltpu.VMEM((LON, 256), BF16)],
        "spectral",
        (
            place,
            rows.reshape(LON, 256),
            jnp.asarray(lon_table(), BF16),
            jnp.asarray(lon_inverse_table(), BF16),
            small,
        ),
        scalars=1,
    )
    back, z1 = lax.optimization_barrier((back.reshape(32, 16, 256), z1))
    z2 = next_pair(z1)
    x2 = swap(z1, "xl")
    back = lax.all_to_all(back, LON_AXES, 0, 0)
    back, z2, x2 = lax.optimization_barrier((back, z2, x2))
    mixed = call(
        inverse_kernel,
        shape((16, 64, 128)),
        [pltpu.VMEM((32, 16, 256), F32)],
        "latitude_back",
        (back, tokens, normed, small),
    )
    mixed, z2 = lax.optimization_barrier((mixed.reshape(8, 2, 64, 128), z2))
    x3 = swap(z2, "xl")
    mixed = lax.all_to_all(mixed, OCT_AXES, 0, 0)
    mixed, x3 = lax.optimization_barrier((mixed, x3))
    own = call(
        second_norm_kernel,
        shape((C, 256)),
        [pltpu.VMEM((C, 256), F32)],
        "second_norm",
        (place, mixed, swap(mixed, "xh"), sums),
        scalars=1,
    )
    own_out, other_out = call(
        mlp_kernel,
        [shape((C, 256), F32), shape((C, 256))],
        [],
        "channel_mlp",
        (packed, z0, z1, z2, x0, x1, x2, x3, own, swap(own, "core")),
        limit=30 << 20,
    )
    keep, send = call(
        core_sum_kernel,
        [shape((512, 256), F32), shape((512, 256))],
        [],
        "core_sum",
        (place, own_out, swap(other_out, "core")),
        scalars=1,
    )
    result = call(
        finish_kernel, shape((8, 2, 64, 128)), [], "finish", (mixed, keep, swap(send, "xh"))
    )
    result = lax.all_to_all(lax.optimization_barrier(result), OCT_AXES, 0, 0)
    return result.reshape(16, 64, 128).transpose(2, 0, 1)


def solution(mesh):
    fine = Mesh(
        mesh.devices.reshape(2, 8, 2, 2, 2, 4), ("zl", "y", "core", "xh", "xl", "zh")
    )
    return jax.shard_map(
        per_device,
        mesh=fine,
        in_specs=(
            P(None, LON_AXES, CH_AXES),
            P(CH_AXES),
            P(None, CH_AXES, None),
            P(None, CH_AXES, None),
            P(CH_AXES),
            P(None, CH_AXES),
            P(CH_AXES, None),
        ),
        out_specs=P(None, LON_AXES, CH_AXES),
        check_vma=False,
    )
```

```python
import math

import jax
import jax.numpy as jnp
import numpy as np
from jax import lax
from jax.experimental import pallas as pl
from jax.experimental.pallas import tpu as pltpu
from jax.sharding import Mesh
from jax.sharding import PartitionSpec as P

EPSILON = 1e-05
THRESHOLD = 0.1
LAT = 128
GAIN_ROW = 416
LON = 512
KW = 256
C = 1024
F32 = jnp.float32
BF16 = jnp.bfloat16
VMEM = pl.BlockSpec(memory_space=pltpu.VMEM)
PARAMS = pltpu.CompilerParams(vmem_limit_bytes=10 << 20)

LON_AXES = ("zl", "y", "core")
CH_AXES = ("xh", "xl", "zh")
NT = (((1,), (1,)), ((), ()))
TN = (((0,), (0,)), ((), ()))


def lat_table():
    lat = np.arange(LAT)
    rows = np.zeros((LAT, LAT))
    for mode in range(LAT // 2):
        phase = 2.0 * math.pi * ((lat * mode) % LAT) / LAT
        rows[2 * mode] = np.cos(phase)
        rows[2 * mode + 1] = np.sin(phase)
    rows[1] = np.cos(math.pi * lat)
    return rows / math.sqrt(LAT)


def lat_pairs():
    table = lat_table().reshape(32, 2, 2, LAT)
    return table.transpose(1, 0, 2, 3).reshape(64, 2 * LAT)


def lon_table():
    phase = 2.0 * math.pi * ((np.arange(KW)[:, None] * np.arange(LON)[None, :]) % LON) / LON
    return np.concatenate([np.cos(phase), np.sin(phase)]) / math.sqrt(LON)


def lon_inverse_table():
    weight = np.where(np.arange(KW) == 0, 1.0, 2.0)
    return lon_table().T * np.concatenate([weight, weight])[None, :]


SIGNS_IN = np.array(
    [
        [[1, 0, 1, 0], [0, -1, 0, 1], [0, -1, 0, -1], [-1, 0, 1, 0]],
        [[0, 1, 0, 1], [1, 0, -1, 0], [1, 0, 1, 0], [0, -1, 0, 1]],
        [[1, 0, 0, 0], [0, 0, 1, 0], [0, -1, 0, 0], [0, 0, 0, -1]],
        [[0, 1, 0, 0], [0, 0, 0, 1], [1, 0, 0, 0], [0, 0, 1, 0]],
    ]
)
SIGNS_OUT = np.array(
    [
        [
            [1, 0, 0, 0, 0, -1, 0, 0],
            [0, -1, 0, 0, -1, 0, 0, 0],
            [0, 0, 1, 0, 0, 0, 0, 1],
            [0, 0, 0, 1, 0, 0, -1, 0],
        ],
        [
            [0, -1, 0, 0, -1, 0, 0, 0],
            [-1, 0, 0, 0, 0, 1, 0, 0],
            [0, 0, 0, 1, 0, 0, -1, 0],
            [0, 0, -1, 0, 0, 0, 0, -1],
        ],
        [
            [1, 0, 0, 0, 0, 0, 0, 0],
            [0, 0, 0, 0, -1, 0, 0, 0],
            [0, 1, 0, 0, 0, 0, 0, 0],
            [0, 0, 0, 0, 0, -1, 0, 0],
        ],
        [
            [0, 0, 0, 0, -1, 0, 0, 0],
            [-1, 0, 0, 0, 0, 0, 0, 0],
            [0, 0, 0, 0, 0, -1, 0, 0],
            [0, -1, 0, 0, 0, 0, 0, 0],
        ],
    ]
)


def sign_rows(signs):
    wide = np.repeat(signs, 64, axis=2)
    return np.pad(wide, ((0, 0), (0, 4), (0, 0)))


def shrink(values):
    return values - jnp.clip(values, -THRESHOLD, THRESHOLD)


def column_of(row):
    size = row.shape[1]
    diagonal = lax.broadcasted_iota(jnp.int32, (size, size), 0) == lax.broadcasted_iota(
        jnp.int32, (size, size), 1
    )
    return jnp.sum(jnp.where(diagonal, row, 0.0), axis=1, keepdims=True)


def setup_kernel(up_ref, down_ref, tokens_ref, gain_ref, packed_ref, sums_ref, up_part, tokens_part, gain_part, sems):
    half = pl.ds(pl.multiple_of(lax.axis_index("core") * 128, 128), 128)
    pairs = [
        (tokens_ref, tokens_part),
        (gain_ref, gain_part),
        (up_ref.at[:, half], up_part),
        (down_ref.at[half], packed_ref.at[1]),
    ]
    copies = [pltpu.make_async_copy(a, b, sems.at[i]) for i, (a, b) in enumerate(pairs)]
    for copy in copies:
        copy.start()
    copies[0].wait()
    copies[1].wait()
    values = tokens_part[...].astype(F32)
    gain = gain_part[...].astype(F32).reshape(1, 64)
    block = jnp.concatenate(
        [
            jnp.sum(values, axis=1),
            jnp.sum(values * values, axis=1),
            jnp.broadcast_to(jnp.concatenate([gain, gain], axis=1), (8, 128)),
        ]
    )
    sums_ref[...] = jnp.broadcast_to(block[None], sums_ref.shape)
    copies[2].wait()
    row = lax.broadcasted_iota(jnp.int32, (128, 128), 0)
    lane = lax.broadcasted_iota(jnp.int32, (128, 128), 1)
    pick = jnp.where(lane == row, 1.0, 0.0).astype(BF16)
    packed_ref[0] = lax.dot_general(pick, up_part[...], NT, preferred_element_type=F32).astype(BF16)
    copies[3].wait()


def setup(*args):
    return pl.pallas_call(
        setup_kernel,
        out_shape=[shape((2, 128, C)), shape((16, 40, 128), F32)],
        in_specs=[pl.BlockSpec(memory_space=pl.ANY)] * 4,
        out_specs=[VMEM] * 2,
        scratch_shapes=[
            pltpu.VMEM((C, 128), BF16),
            pltpu.VMEM((16, 64, 128), BF16),
            pltpu.VMEM((64,), BF16),
            pltpu.SemaphoreType.DMA((4,)),
        ],
        compiler_params=pltpu.CompilerParams(vmem_limit_bytes=60 << 20),
        name="setup",
    )(*args)


def forward_kernel(sums_ref, tokens_ref, small_ref, normed_ref, out_ref, twice, wide):
    total = jnp.sum(sums_ref[:, :32, :], axis=0)
    centre = total[:16] / C
    spread = total[16:] / C - centre * centre
    scale = lax.rsqrt(spread + EPSILON)
    gain = column_of(small_ref[GAIN_ROW : GAIN_ROW + 1, :64].astype(F32))
    twice[...] = jnp.zeros_like(twice)
    table = small_ref[:64]
    for w in range(16):
        values = tokens_ref[w].astype(F32)
        normed = ((values - centre[w : w + 1]) * scale[w : w + 1] * gain).astype(BF16)
        normed_ref[w] = normed
        slot = w % 2
        twice[slot, :64, :LAT] = normed
        twice[slot, 64:, LAT:] = normed
        rows = lax.dot_general(table, twice[slot], NT, preferred_element_type=F32)
        wide[:, w, :128] = rows[:32]
        wide[:, w, 128:] = rows[32:]
    out_ref[...] = wide[...].astype(BF16)


def spectral_kernel(rows_ref, lon_ref, inverse_ref, small_ref, out_ref, modes):
    waves = jnp.dot(lon_ref[...], rows_ref[...], preferred_element_type=F32).astype(BF16)
    at_edge = lax.axis_index("zl") + lax.axis_index("y") + lax.axis_index("core") == 0
    row = lax.broadcasted_iota(jnp.int32, (256, 8), 0) // 64
    spot = lax.broadcasted_iota(jnp.int32, (256, 8), 1)
    blocks = jnp.where(row == spot, 1.0, 0.0).astype(BF16)
    down64 = lax.broadcasted_iota(jnp.int32, (256, 64), 0) % 64
    stack = jnp.where(down64 == lax.broadcasted_iota(jnp.int32, (256, 64), 1), 1.0, 0.0).astype(BF16)

    def tables(weights, signs, columns):
        lane = lax.broadcasted_iota(jnp.int32, (64, columns), 1) % 64
        spread = jnp.where(lane == lax.broadcasted_iota(jnp.int32, (64, columns), 0), 1.0, 0.0)
        spread = spread.astype(BF16)
        tiles = []
        for part in range(2):
            tall = jnp.dot(stack, weights[part], preferred_element_type=F32).astype(BF16)
            tiles.append(jnp.dot(tall, spread, preferred_element_type=F32))
        found = []
        for kind in (0, 2):
            mask = [
                jnp.dot(blocks, signs[kind + part], preferred_element_type=F32)
                for part in range(2)
            ]
            found.append(tiles[0] * mask[0] + tiles[1] * mask[1])
        plain, edge = found
        return [jnp.where(at_edge, edge, plain).astype(BF16), plain.astype(BF16)]

    def rows_of(start, count):
        return small_ref[start : start + count]

    first = [rows_of(160 + 64 * part, 64)[:, :64] for part in range(2)]
    second = [rows_of(288 + 64 * part, 64)[:, :64] for part in range(2)]
    signs_in = [rows_of(64 + 8 * kind, 8) for kind in range(4)]
    signs_out = [
        jnp.concatenate([rows_of(96 + 8 * kind, 8), rows_of(128 + 8 * kind, 8)], axis=1)
        for kind in range(4)
    ]
    mix_in = tables(first, signs_in, 256)
    mix_out = tables(second, signs_out, 512)
    for pair in range(2):
        lanes = slice(pair * 128, pair * 128 + 128)
        middle = jnp.dot(waves[:KW, lanes], mix_in[pair][:128], preferred_element_type=F32)
        middle += jnp.dot(waves[KW:, lanes], mix_in[pair][128:], preferred_element_type=F32)
        middle = jnp.maximum(middle, 0.0).astype(BF16)
        back = shrink(jnp.dot(middle, mix_out[pair], preferred_element_type=F32))
        modes[:KW, lanes] = (back[:, :128] + back[:, 128:256]).astype(BF16)
        modes[KW:, lanes] = (back[:, 256:384] + back[:, 384:]).astype(BF16)
    out_ref[...] = jnp.dot(inverse_ref[...], modes[...], preferred_element_type=F32).astype(BF16)


def inverse_kernel(rows_ref, tokens_ref, normed_ref, small_ref, mixed_ref, wide):
    wide[...] = rows_ref[...].astype(F32)
    table = small_ref[:64]
    for w in range(16):
        rows = jnp.concatenate([wide[:, w, :128], wide[:, w, 128:]]).astype(BF16)
        both = lax.dot_general(rows, table, TN, preferred_element_type=F32)
        filtered = (both[:64, :LAT] + both[64:, LAT:]).astype(BF16).astype(F32)
        mixed = tokens_ref[w].astype(F32) + normed_ref[w].astype(F32) + filtered
        mixed_ref[0, w // 2, w % 2] = mixed.astype(BF16)
        mixed_ref[1, w // 2, w % 2] = mixed.astype(BF16)


def second_norm_kernel(mixed_ref, sums_ref, out_ref):
    for w in range(2):
        wide = mixed_ref[:, w].astype(F32).reshape(C, 128)
        mean = jnp.sum(wide, axis=0, keepdims=True) / C
        power = jnp.sum(wide * wide, axis=0, keepdims=True) / C - mean * mean
        scale = lax.rsqrt(power + EPSILON)
        for block in range(16):
            rows = slice(block * 64, block * 64 + 64)
            gain = column_of(sums_ref[block, 32:33, :64])
            values = mixed_ref[block, w].astype(F32)
            out = (values - mean) * scale * gain
            out_ref[rows, w * 128 : w * 128 + 128] = out.astype(BF16)


def mlp_kernel(*refs):
    p0, z0, z1, z2, x0, x12, x3, own_ref, other_ref, own_out, other_out = refs
    pieces = [p0, z0, z1, z2, x0, x12.at[0], x12.at[1], x3]
    group = jnp.concatenate([own_ref[...], other_ref[...]], axis=1)
    total = None
    for first, second in zip(pieces[0::2], pieces[1::2]):
        up = jnp.concatenate([first[0], second[0]])
        down = jnp.concatenate([first[1], second[1]])
        upward = jnp.dot(up, group, preferred_element_type=F32)
        hidden = jax.nn.gelu(upward).astype(BF16)
        found = lax.dot_general(down, hidden, TN, preferred_element_type=F32)
        total = found if total is None else total + found
    own_out[...] = total[:, :256]
    other_out[...] = total[:, 256:].astype(BF16)


def core_sum_kernel(own_ref, other_ref, keep_ref, send_ref):
    xh = lax.axis_index("xh")
    mine = pl.ds(pl.multiple_of(xh * 512, 512), 512)
    theirs = pl.ds(pl.multiple_of((1 - xh) * 512, 512), 512)
    keep_ref[...] = own_ref[mine] + other_ref[mine].astype(F32)
    send_ref[...] = (own_ref[theirs] + other_ref[theirs].astype(F32)).astype(BF16)


def finish_kernel(wide_ref, keep_ref, other_ref, out_ref):
    xh = lax.axis_index("xh")
    for d in range(8):
        rows = slice(d * 64, d * 64 + 64)
        branch = keep_ref[rows] + other_ref[rows].astype(F32)
        for w in range(2):
            sums = wide_ref[xh * 8 + d, w].astype(F32) + branch[:, w * 128 : w * 128 + 128]
            out_ref[d, w] = sums.astype(BF16)


def call(kernel, shapes, scratch, name, args, limit=10 << 20):
    specs = [VMEM] * len(args)
    many = isinstance(shapes, list)
    return pl.pallas_call(
        kernel,
        out_shape=shapes,
        in_specs=specs,
        out_specs=[VMEM] * len(shapes) if many else VMEM,
        scratch_shapes=scratch,
        compiler_params=pltpu.CompilerParams(vmem_limit_bytes=limit),
        name=name,
    )(*args)


def shape(dims, kind=BF16):
    return jax.ShapeDtypeStruct(dims, kind)


def swap(values, axis):
    return lax.ppermute(values, axis, [(0, 1), (1, 0)])


def next_pair(values):
    pairs = []
    for zh in range(4):
        pairs.append((4 + zh, (zh + 1) % 4))
        pairs.append((zh, 4 + (zh - 1) % 4))
    return lax.ppermute(values, ("zl", "zh"), pairs)


def per_device(grid_state, first_gain, spectral_first, spectral_second, second_gain, up_weight, down_weight):
    tokens = grid_state.transpose(1, 2, 0)
    packed, sums = setup(up_weight, down_weight, tokens, second_gain)
    z0 = next_pair(packed)
    x0 = swap(packed, "xl")
    sums = lax.all_to_all(sums, CH_AXES, 0, 0)
    signs_out = sign_rows(SIGNS_OUT).reshape(32, 512)
    small = jnp.concatenate(
        [
            jnp.asarray(lat_pairs(), BF16),
            jnp.asarray(sign_rows(SIGNS_IN).reshape(32, 256), BF16),
            jnp.asarray(signs_out[:, :256], BF16),
            jnp.asarray(signs_out[:, 256:], BF16),
            jnp.pad(spectral_first.reshape(128, 64), ((0, 0), (0, 192))),
            jnp.pad(spectral_second.reshape(128, 64), ((0, 0), (0, 192))),
            jnp.pad(first_gain[None], ((0, 15), (0, 192))),
        ]
    )
    sums, small, z0, x0 = lax.optimization_barrier((sums, small, z0, x0))
    normed, rows = call(
        forward_kernel,
        [shape((16, 64, 128)), shape((32, 16, 256))],
        [pltpu.VMEM((2, 128, 256), BF16), pltpu.VMEM((32, 16, 256), F32)],
        "norm_latitude",
        (sums, tokens, small),
    )
    rows, z0 = lax.optimization_barrier((rows, z0))
    z1 = swap(z0, "zl")
    rows = lax.all_to_all(rows, LON_AXES, 0, 0)
    rows, z1 = lax.optimization_barrier((rows, z1))
    x12 = swap(jnp.stack([z0, z1]), "xl")
    back = call(
        spectral_kernel,
        shape((LON, 256)),
        [pltpu.VMEM((LON, 256), BF16)],
        "spectral",
        (
            rows.reshape(LON, 256),
            jnp.asarray(lon_table(), BF16),
            jnp.asarray(lon_inverse_table(), BF16),
            small,
        ),
    )
    back, z1 = lax.optimization_barrier((back.reshape(32, 16, 256), z1))
    z2 = next_pair(z1)
    back = lax.all_to_all(back, LON_AXES, 0, 0)
    back, z2, x12 = lax.optimization_barrier((back, z2, x12))
    mixed = call(
        inverse_kernel,
        shape((2, 8, 2, 64, 128)),
        [pltpu.VMEM((32, 16, 256), F32)],
        "latitude_back",
        (back, tokens, normed, small),
    )
    mixed, z2 = lax.optimization_barrier((mixed, z2))
    x3 = swap(z2, "xl")
    wide = lax.all_to_all(mixed.reshape(16, 2, 64, 128), CH_AXES, 0, 0)
    wide = lax.optimization_barrier(wide)
    own = call(second_norm_kernel, shape((C, 256)), [], "second_norm", (wide, sums))
    own_out, other_out = call(
        mlp_kernel,
        [shape((C, 256), F32), shape((C, 256))],
        [],
        "channel_mlp",
        (packed, z0, z1, z2, x0, x12, x3, own, swap(own, "core")),
        limit=30 << 20,
    )
    keep, send = call(
        core_sum_kernel,
        [shape((512, 256), F32), shape((512, 256))],
        [],
        "core_sum",
        (own_out, swap(other_out, "core")),
    )
    result = call(finish_kernel, shape((8, 2, 64, 128)), [], "finish", (wide, keep, swap(send, "xh")))
    result = lax.all_to_all(lax.optimization_barrier(result), ("xl", "zh"), 0, 0)
    return result.reshape(16, 64, 128).transpose(2, 0, 1)


def solution(mesh):
    fine = Mesh(
        mesh.devices.reshape(2, 8, 2, 2, 2, 4), ("zl", "y", "core", "xh", "xl", "zh")
    )
    return jax.shard_map(
        per_device,
        mesh=fine,
        in_specs=(
            P(None, LON_AXES, CH_AXES),
            P(CH_AXES),
            P(None, CH_AXES, None),
            P(None, CH_AXES, None),
            P(CH_AXES),
            P(None, CH_AXES),
            P(CH_AXES, None),
        ),
        out_specs=P(None, LON_AXES, CH_AXES),
        check_vma=False,
    )
```

```python
import math

import jax
import jax.numpy as jnp
import numpy as np
from jax import lax
from jax.experimental import pallas as pl
from jax.experimental.pallas import tpu as pltpu
from jax.sharding import Mesh
from jax.sharding import PartitionSpec as P

EPSILON = 1e-05
THRESHOLD = 0.1
LAT = 128
GAIN_ROW = 416
LON = 512
KW = 256
C = 1024
F32 = jnp.float32
BF16 = jnp.bfloat16
VMEM = pl.BlockSpec(memory_space=pltpu.VMEM)
PARAMS = pltpu.CompilerParams(vmem_limit_bytes=10 << 20)

LON_AXES = ("zl", "y", "core")
CH_AXES = ("xh", "xl", "zh")
NT = (((1,), (1,)), ((), ()))
TN = (((0,), (0,)), ((), ()))


def lat_table():
    lat = np.arange(LAT)
    rows = np.zeros((LAT, LAT))
    for mode in range(LAT // 2):
        phase = 2.0 * math.pi * ((lat * mode) % LAT) / LAT
        rows[2 * mode] = np.cos(phase)
        rows[2 * mode + 1] = np.sin(phase)
    rows[1] = np.cos(math.pi * lat)
    return rows / math.sqrt(LAT)


def lat_pairs():
    table = lat_table().reshape(32, 2, 2, LAT)
    return table.transpose(1, 0, 2, 3).reshape(64, 2 * LAT)


def lon_table():
    phase = 2.0 * math.pi * ((np.arange(KW)[:, None] * np.arange(LON)[None, :]) % LON) / LON
    return np.concatenate([np.cos(phase), np.sin(phase)]) / math.sqrt(LON)


def lon_inverse_table():
    weight = np.where(np.arange(KW) == 0, 1.0, 2.0)
    return lon_table().T * np.concatenate([weight, weight])[None, :]


SIGNS_IN = np.array(
    [
        [[1, 0, 1, 0], [0, -1, 0, 1], [0, -1, 0, -1], [-1, 0, 1, 0]],
        [[0, 1, 0, 1], [1, 0, -1, 0], [1, 0, 1, 0], [0, -1, 0, 1]],
        [[1, 0, 0, 0], [0, 0, 1, 0], [0, -1, 0, 0], [0, 0, 0, -1]],
        [[0, 1, 0, 0], [0, 0, 0, 1], [1, 0, 0, 0], [0, 0, 1, 0]],
    ]
)
SIGNS_OUT = np.array(
    [
        [
            [1, 0, 0, 0, 0, -1, 0, 0],
            [0, -1, 0, 0, -1, 0, 0, 0],
            [0, 0, 1, 0, 0, 0, 0, 1],
            [0, 0, 0, 1, 0, 0, -1, 0],
        ],
        [
            [0, -1, 0, 0, -1, 0, 0, 0],
            [-1, 0, 0, 0, 0, 1, 0, 0],
            [0, 0, 0, 1, 0, 0, -1, 0],
            [0, 0, -1, 0, 0, 0, 0, -1],
        ],
        [
            [1, 0, 0, 0, 0, 0, 0, 0],
            [0, 0, 0, 0, -1, 0, 0, 0],
            [0, 1, 0, 0, 0, 0, 0, 0],
            [0, 0, 0, 0, 0, -1, 0, 0],
        ],
        [
            [0, 0, 0, 0, -1, 0, 0, 0],
            [-1, 0, 0, 0, 0, 0, 0, 0],
            [0, 0, 0, 0, 0, -1, 0, 0],
            [0, -1, 0, 0, 0, 0, 0, 0],
        ],
    ]
)


def sign_rows(signs):
    wide = np.repeat(signs, 64, axis=2)
    return np.pad(wide, ((0, 0), (0, 4), (0, 0)))


def shrink(values):
    return values - jnp.clip(values, -THRESHOLD, THRESHOLD)


def column_of(row):
    size = row.shape[1]
    diagonal = lax.broadcasted_iota(jnp.int32, (size, size), 0) == lax.broadcasted_iota(
        jnp.int32, (size, size), 1
    )
    return jnp.sum(jnp.where(diagonal, row, 0.0), axis=1, keepdims=True)


def setup_kernel(up_ref, down_ref, tokens_ref, gain_ref, packed_ref, sums_ref, up_part, tokens_part, gain_part, sems):
    half = pl.ds(pl.multiple_of(lax.axis_index("core") * 128, 128), 128)
    pairs = [
        (tokens_ref, tokens_part),
        (gain_ref, gain_part),
        (up_ref.at[:, half], up_part),
        (down_ref.at[half], packed_ref.at[1]),
    ]
    copies = [pltpu.make_async_copy(a, b, sems.at[i]) for i, (a, b) in enumerate(pairs)]
    for copy in copies:
        copy.start()
    copies[0].wait()
    copies[1].wait()
    values = tokens_part[...].astype(F32)
    gain = gain_part[...].astype(F32).reshape(1, 64)
    block = jnp.concatenate(
        [
            jnp.sum(values, axis=1),
            jnp.sum(values * values, axis=1),
            jnp.broadcast_to(jnp.concatenate([gain, gain], axis=1), (8, 128)),
        ]
    )
    sums_ref[...] = jnp.broadcast_to(block[None], sums_ref.shape)
    copies[2].wait()
    row = lax.broadcasted_iota(jnp.int32, (128, 128), 0)
    lane = lax.broadcasted_iota(jnp.int32, (128, 128), 1)
    pick = jnp.where(lane == row, 1.0, 0.0).astype(BF16)
    packed_ref[0] = lax.dot_general(pick, up_part[...], NT, preferred_element_type=F32).astype(BF16)
    copies[3].wait()


def setup(*args):
    return pl.pallas_call(
        setup_kernel,
        out_shape=[shape((2, 128, C)), shape((16, 40, 128), F32)],
        in_specs=[pl.BlockSpec(memory_space=pl.ANY)] * 4,
        out_specs=[VMEM] * 2,
        scratch_shapes=[
            pltpu.VMEM((C, 128), BF16),
            pltpu.VMEM((16, 64, 128), BF16),
            pltpu.VMEM((64,), BF16),
            pltpu.SemaphoreType.DMA((4,)),
        ],
        compiler_params=pltpu.CompilerParams(vmem_limit_bytes=60 << 20),
        name="setup",
    )(*args)


def forward_kernel(sums_ref, tokens_ref, small_ref, normed_ref, out_ref, twice, wide):
    total = jnp.sum(sums_ref[:, :32, :], axis=0)
    centre = total[:16] / C
    spread = total[16:] / C - centre * centre
    scale = lax.rsqrt(spread + EPSILON)
    gain = column_of(small_ref[GAIN_ROW : GAIN_ROW + 1, :64].astype(F32))
    twice[...] = jnp.zeros_like(twice)
    table = small_ref[:64]
    for w in range(16):
        values = tokens_ref[w].astype(F32)
        normed = ((values - centre[w : w + 1]) * scale[w : w + 1] * gain).astype(BF16)
        normed_ref[w] = normed
        slot = w % 2
        twice[slot, :64, :LAT] = normed
        twice[slot, 64:, LAT:] = normed
        rows = lax.dot_general(table, twice[slot], NT, preferred_element_type=F32)
        wide[:, w, :128] = rows[:32]
        wide[:, w, 128:] = rows[32:]
    out_ref[...] = wide[...].astype(BF16)


def spectral_kernel(rows_ref, lon_ref, inverse_ref, small_ref, out_ref, modes):
    waves = jnp.dot(lon_ref[...], rows_ref[...], preferred_element_type=F32).astype(BF16)
    at_edge = lax.axis_index("zl") + lax.axis_index("y") + lax.axis_index("core") == 0
    row = lax.broadcasted_iota(jnp.int32, (256, 8), 0) // 64
    spot = lax.broadcasted_iota(jnp.int32, (256, 8), 1)
    blocks = jnp.where(row == spot, 1.0, 0.0).astype(BF16)
    down64 = lax.broadcasted_iota(jnp.int32, (256, 64), 0) % 64
    stack = jnp.where(down64 == lax.broadcasted_iota(jnp.int32, (256, 64), 1), 1.0, 0.0).astype(BF16)

    def tables(weights, signs, columns):
        lane = lax.broadcasted_iota(jnp.int32, (64, columns), 1) % 64
        spread = jnp.where(lane == lax.broadcasted_iota(jnp.int32, (64, columns), 0), 1.0, 0.0)
        spread = spread.astype(BF16)
        tiles = []
        for part in range(2):
            tall = jnp.dot(stack, weights[part], preferred_element_type=F32).astype(BF16)
            tiles.append(jnp.dot(tall, spread, preferred_element_type=F32))
        found = []
        for kind in (0, 2):
            mask = [
                jnp.dot(blocks, signs[kind + part], preferred_element_type=F32)
                for part in range(2)
            ]
            found.append(tiles[0] * mask[0] + tiles[1] * mask[1])
        plain, edge = found
        return [jnp.where(at_edge, edge, plain).astype(BF16), plain.astype(BF16)]

    def rows_of(start, count):
        return small_ref[start : start + count]

    first = [rows_of(160 + 64 * part, 64)[:, :64] for part in range(2)]
    second = [rows_of(288 + 64 * part, 64)[:, :64] for part in range(2)]
    signs_in = [rows_of(64 + 8 * kind, 8) for kind in range(4)]
    signs_out = [
        jnp.concatenate([rows_of(96 + 8 * kind, 8), rows_of(128 + 8 * kind, 8)], axis=1)
        for kind in range(4)
    ]
    mix_in = tables(first, signs_in, 256)
    mix_out = tables(second, signs_out, 512)
    for pair in range(2):
        lanes = slice(pair * 128, pair * 128 + 128)
        middle = jnp.dot(waves[:KW, lanes], mix_in[pair][:128], preferred_element_type=F32)
        middle += jnp.dot(waves[KW:, lanes], mix_in[pair][128:], preferred_element_type=F32)
        middle = jnp.maximum(middle, 0.0).astype(BF16)
        back = shrink(jnp.dot(middle, mix_out[pair], preferred_element_type=F32))
        modes[:KW, lanes] = (back[:, :128] + back[:, 128:256]).astype(BF16)
        modes[KW:, lanes] = (back[:, 256:384] + back[:, 384:]).astype(BF16)
    out_ref[...] = jnp.dot(inverse_ref[...], modes[...], preferred_element_type=F32).astype(BF16)


def inverse_kernel(rows_ref, tokens_ref, normed_ref, small_ref, mixed_ref, wide):
    wide[...] = rows_ref[...].astype(F32)
    table = small_ref[:64]
    for w in range(16):
        rows = jnp.concatenate([wide[:, w, :128], wide[:, w, 128:]]).astype(BF16)
        both = lax.dot_general(rows, table, TN, preferred_element_type=F32)
        filtered = (both[:64, :LAT] + both[64:, LAT:]).astype(BF16).astype(F32)
        mixed = tokens_ref[w].astype(F32) + normed_ref[w].astype(F32) + filtered
        mixed_ref[0, w // 2, w % 2] = mixed.astype(BF16)
        mixed_ref[1, w // 2, w % 2] = mixed.astype(BF16)


def second_norm_kernel(mixed_ref, sums_ref, out_ref):
    for w in range(2):
        wide = mixed_ref[:, w].astype(F32).reshape(C, 128)
        mean = jnp.sum(wide, axis=0, keepdims=True) / C
        power = jnp.sum(wide * wide, axis=0, keepdims=True) / C - mean * mean
        scale = lax.rsqrt(power + EPSILON)
        for block in range(16):
            rows = slice(block * 64, block * 64 + 64)
            gain = column_of(sums_ref[block, 32:33, :64])
            values = mixed_ref[block, w].astype(F32)
            out = (values - mean) * scale * gain
            out_ref[rows, w * 128 : w * 128 + 128] = out.astype(BF16)


def mlp_kernel(*refs):
    p0, z0, z1, z2, x0, x12, x3, own_ref, other_ref, own_out, other_out = refs
    pieces = [p0, z0, z1, z2, x0, x12.at[0], x12.at[1], x3]
    group = jnp.concatenate([own_ref[...], other_ref[...]], axis=1)
    total = None
    for first, second in zip(pieces[0::2], pieces[1::2]):
        up = jnp.concatenate([first[0], second[0]])
        down = jnp.concatenate([first[1], second[1]])
        upward = jnp.dot(up, group, preferred_element_type=F32)
        hidden = jax.nn.gelu(upward).astype(BF16)
        found = lax.dot_general(down, hidden, TN, preferred_element_type=F32)
        total = found if total is None else total + found
    own_out[...] = total[:, :256]
    other_out[...] = total[:, 256:].astype(BF16)


def core_sum_kernel(own_ref, other_ref, keep_ref, send_ref):
    xh = lax.axis_index("xh")
    mine = pl.ds(pl.multiple_of(xh * 512, 512), 512)
    theirs = pl.ds(pl.multiple_of((1 - xh) * 512, 512), 512)
    keep_ref[...] = own_ref[mine] + other_ref[mine].astype(F32)
    send_ref[...] = (own_ref[theirs] + other_ref[theirs].astype(F32)).astype(BF16)


def finish_kernel(wide_ref, keep_ref, other_ref, out_ref):
    xh = lax.axis_index("xh")
    for d in range(8):
        rows = slice(d * 64, d * 64 + 64)
        branch = keep_ref[rows] + other_ref[1 - xh, rows].astype(F32)
        for w in range(2):
            sums = wide_ref[xh * 8 + d, w].astype(F32) + branch[:, w * 128 : w * 128 + 128]
            out_ref[d, w] = sums.astype(BF16)


def call(kernel, shapes, scratch, name, args, limit=10 << 20):
    specs = [VMEM] * len(args)
    many = isinstance(shapes, list)
    return pl.pallas_call(
        kernel,
        out_shape=shapes,
        in_specs=specs,
        out_specs=[VMEM] * len(shapes) if many else VMEM,
        scratch_shapes=scratch,
        compiler_params=pltpu.CompilerParams(vmem_limit_bytes=limit),
        name=name,
    )(*args)


def shape(dims, kind=BF16):
    return jax.ShapeDtypeStruct(dims, kind)


def swap(values, axis):
    return lax.ppermute(values, axis, [(0, 1), (1, 0)])


def next_pair(values):
    pairs = []
    for zh in range(4):
        pairs.append((4 + zh, (zh + 1) % 4))
        pairs.append((zh, 4 + (zh - 1) % 4))
    return lax.ppermute(values, ("zl", "zh"), pairs)


def per_device(grid_state, first_gain, spectral_first, spectral_second, second_gain, up_weight, down_weight):
    tokens = grid_state.transpose(1, 2, 0)
    packed, sums = setup(up_weight, down_weight, tokens, second_gain)
    z0 = next_pair(packed)
    x0 = swap(packed, "xl")
    sums = lax.all_to_all(sums, CH_AXES, 0, 0)
    signs_out = sign_rows(SIGNS_OUT).reshape(32, 512)
    small = jnp.concatenate(
        [
            jnp.asarray(lat_pairs(), BF16),
            jnp.asarray(sign_rows(SIGNS_IN).reshape(32, 256), BF16),
            jnp.asarray(signs_out[:, :256], BF16),
            jnp.asarray(signs_out[:, 256:], BF16),
            jnp.pad(spectral_first.reshape(128, 64), ((0, 0), (0, 192))),
            jnp.pad(spectral_second.reshape(128, 64), ((0, 0), (0, 192))),
            jnp.pad(first_gain[None], ((0, 15), (0, 192))),
        ]
    )
    sums, small, z0, x0 = lax.optimization_barrier((sums, small, z0, x0))
    normed, rows = call(
        forward_kernel,
        [shape((16, 64, 128)), shape((32, 16, 256))],
        [pltpu.VMEM((2, 128, 256), BF16), pltpu.VMEM((32, 16, 256), F32)],
        "norm_latitude",
        (sums, tokens, small),
    )
    rows, z0 = lax.optimization_barrier((rows, z0))
    z1 = swap(z0, "zl")
    rows = lax.all_to_all(rows, LON_AXES, 0, 0)
    rows, z1 = lax.optimization_barrier((rows, z1))
    x12 = swap(jnp.stack([z0, z1]), "xl")
    back = call(
        spectral_kernel,
        shape((LON, 256)),
        [pltpu.VMEM((LON, 256), BF16)],
        "spectral",
        (
            rows.reshape(LON, 256),
            jnp.asarray(lon_table(), BF16),
            jnp.asarray(lon_inverse_table(), BF16),
            small,
        ),
    )
    back, z1 = lax.optimization_barrier((back.reshape(32, 16, 256), z1))
    z2 = next_pair(z1)
    back = lax.all_to_all(back, LON_AXES, 0, 0)
    back, z2, x12 = lax.optimization_barrier((back, z2, x12))
    mixed = call(
        inverse_kernel,
        shape((2, 8, 2, 64, 128)),
        [pltpu.VMEM((32, 16, 256), F32)],
        "latitude_back",
        (back, tokens, normed, small),
    )
    mixed, z2 = lax.optimization_barrier((mixed, z2))
    x3 = swap(z2, "xl")
    wide = lax.all_to_all(mixed.reshape(16, 2, 64, 128), CH_AXES, 0, 0)
    wide = lax.optimization_barrier(wide)
    own = call(second_norm_kernel, shape((C, 256)), [], "second_norm", (wide, sums))
    own_out, other_out = call(
        mlp_kernel,
        [shape((C, 256), F32), shape((C, 256))],
        [],
        "channel_mlp",
        (packed, z0, z1, z2, x0, x12, x3, own, swap(own, "core")),
        limit=30 << 20,
    )
    keep, send = call(
        core_sum_kernel,
        [shape((512, 256), F32), shape((512, 256))],
        [],
        "core_sum",
        (own_out, swap(other_out, "core")),
    )
    result = call(finish_kernel, shape((8, 2, 64, 128)), [], "finish", (wide, keep, lax.all_gather(send, "xh", axis=0)))
    result = lax.all_to_all(lax.optimization_barrier(result), ("xl", "zh"), 0, 0)
    return result.reshape(16, 64, 128).transpose(2, 0, 1)


def solution(mesh):
    fine = Mesh(
        mesh.devices.reshape(2, 8, 2, 2, 2, 4), ("zl", "y", "core", "xh", "xl", "zh")
    )
    return jax.shard_map(
        per_device,
        mesh=fine,
        in_specs=(
            P(None, LON_AXES, CH_AXES),
            P(CH_AXES),
            P(None, CH_AXES, None),
            P(None, CH_AXES, None),
            P(CH_AXES),
            P(None, CH_AXES),
            P(CH_AXES, None),
        ),
        out_specs=P(None, LON_AXES, CH_AXES),
        check_vma=False,
    )
```

```python
import math

import jax
import jax.numpy as jnp
import numpy as np
from jax import lax
from jax.experimental import pallas as pl
from jax.experimental.pallas import tpu as pltpu
from jax.sharding import Mesh
from jax.sharding import PartitionSpec as P

EPSILON = 1e-05
THRESHOLD = 0.1
LAT = 128
GAIN_ROW = 416
LON = 512
KW = 256
C = 1024
F32 = jnp.float32
BF16 = jnp.bfloat16
VMEM = pl.BlockSpec(memory_space=pltpu.VMEM)
PARAMS = pltpu.CompilerParams(vmem_limit_bytes=10 << 20)

LON_AXES = ("zl", "y", "core")
CH_AXES = ("xh", "xl", "zh")
NT = (((1,), (1,)), ((), ()))
TN = (((0,), (0,)), ((), ()))


def lat_table():
    lat = np.arange(LAT)
    rows = np.zeros((LAT, LAT))
    for mode in range(LAT // 2):
        phase = 2.0 * math.pi * ((lat * mode) % LAT) / LAT
        rows[2 * mode] = np.cos(phase)
        rows[2 * mode + 1] = np.sin(phase)
    rows[1] = np.cos(math.pi * lat)
    return rows / math.sqrt(LAT)


def lat_pairs():
    table = lat_table().reshape(32, 2, 2, LAT)
    return table.transpose(1, 0, 2, 3).reshape(64, 2 * LAT)


def lon_table():
    phase = 2.0 * math.pi * ((np.arange(KW)[:, None] * np.arange(LON)[None, :]) % LON) / LON
    return np.concatenate([np.cos(phase), np.sin(phase)]) / math.sqrt(LON)


def lon_inverse_table():
    weight = np.where(np.arange(KW) == 0, 1.0, 2.0)
    return lon_table().T * np.concatenate([weight, weight])[None, :]


SIGNS_IN = np.array(
    [
        [[1, 0, 1, 0], [0, -1, 0, 1], [0, -1, 0, -1], [-1, 0, 1, 0]],
        [[0, 1, 0, 1], [1, 0, -1, 0], [1, 0, 1, 0], [0, -1, 0, 1]],
        [[1, 0, 0, 0], [0, 0, 1, 0], [0, -1, 0, 0], [0, 0, 0, -1]],
        [[0, 1, 0, 0], [0, 0, 0, 1], [1, 0, 0, 0], [0, 0, 1, 0]],
    ]
)
SIGNS_OUT = np.array(
    [
        [
            [1, 0, 0, 0, 0, -1, 0, 0],
            [0, -1, 0, 0, -1, 0, 0, 0],
            [0, 0, 1, 0, 0, 0, 0, 1],
            [0, 0, 0, 1, 0, 0, -1, 0],
        ],
        [
            [0, -1, 0, 0, -1, 0, 0, 0],
            [-1, 0, 0, 0, 0, 1, 0, 0],
            [0, 0, 0, 1, 0, 0, -1, 0],
            [0, 0, -1, 0, 0, 0, 0, -1],
        ],
        [
            [1, 0, 0, 0, 0, 0, 0, 0],
            [0, 0, 0, 0, -1, 0, 0, 0],
            [0, 1, 0, 0, 0, 0, 0, 0],
            [0, 0, 0, 0, 0, -1, 0, 0],
        ],
        [
            [0, 0, 0, 0, -1, 0, 0, 0],
            [-1, 0, 0, 0, 0, 0, 0, 0],
            [0, 0, 0, 0, 0, -1, 0, 0],
            [0, -1, 0, 0, 0, 0, 0, 0],
        ],
    ]
)


def sign_rows(signs):
    wide = np.repeat(signs, 64, axis=2)
    return np.pad(wide, ((0, 0), (0, 4), (0, 0)))


def shrink(values):
    return values - jnp.clip(values, -THRESHOLD, THRESHOLD)


def column_of(row):
    size = row.shape[1]
    diagonal = lax.broadcasted_iota(jnp.int32, (size, size), 0) == lax.broadcasted_iota(
        jnp.int32, (size, size), 1
    )
    return jnp.sum(jnp.where(diagonal, row, 0.0), axis=1, keepdims=True)


def setup_kernel(up_ref, down_ref, tokens_ref, gain_ref, packed_ref, sums_ref, up_part, tokens_part, gain_part, sems):
    half = pl.ds(pl.multiple_of(lax.axis_index("core") * 128, 128), 128)
    pairs = [
        (tokens_ref, tokens_part),
        (gain_ref, gain_part),
        (up_ref.at[:, half], up_part),
        (down_ref.at[half], packed_ref.at[1]),
    ]
    copies = [pltpu.make_async_copy(a, b, sems.at[i]) for i, (a, b) in enumerate(pairs)]
    for copy in copies:
        copy.start()
    copies[0].wait()
    copies[1].wait()
    values = tokens_part[...].astype(F32)
    gain = gain_part[...].astype(F32).reshape(1, 64)
    block = jnp.concatenate(
        [
            jnp.sum(values, axis=1),
            jnp.sum(values * values, axis=1),
            jnp.broadcast_to(jnp.concatenate([gain, gain], axis=1), (8, 128)),
        ]
    )
    sums_ref[...] = jnp.broadcast_to(block[None], sums_ref.shape)
    copies[2].wait()
    row = lax.broadcasted_iota(jnp.int32, (128, 128), 0)
    lane = lax.broadcasted_iota(jnp.int32, (128, 128), 1)
    pick = jnp.where(lane == row, 1.0, 0.0).astype(BF16)
    packed_ref[0] = lax.dot_general(pick, up_part[...], NT, preferred_element_type=F32).astype(BF16)
    copies[3].wait()


def setup(*args):
    return pl.pallas_call(
        setup_kernel,
        out_shape=[shape((2, 128, C)), shape((16, 40, 128), F32)],
        in_specs=[pl.BlockSpec(memory_space=pl.ANY)] * 4,
        out_specs=[VMEM] * 2,
        scratch_shapes=[
            pltpu.VMEM((C, 128), BF16),
            pltpu.VMEM((16, 64, 128), BF16),
            pltpu.VMEM((64,), BF16),
            pltpu.SemaphoreType.DMA((4,)),
        ],
        compiler_params=pltpu.CompilerParams(vmem_limit_bytes=60 << 20),
        name="setup",
    )(*args)


def forward_kernel(sums_ref, tokens_ref, small_ref, normed_ref, out_ref, twice, wide):
    total = jnp.sum(sums_ref[:, :32, :], axis=0)
    centre = total[:16] / C
    spread = total[16:] / C - centre * centre
    scale = lax.rsqrt(spread + EPSILON)
    gain = column_of(small_ref[GAIN_ROW : GAIN_ROW + 1, :64].astype(F32))
    twice[...] = jnp.zeros_like(twice)
    table = small_ref[:64]
    for w in range(16):
        values = tokens_ref[w].astype(F32)
        normed = ((values - centre[w : w + 1]) * scale[w : w + 1] * gain).astype(BF16)
        normed_ref[w] = normed
        slot = w % 2
        twice[slot, :64, :LAT] = normed
        twice[slot, 64:, LAT:] = normed
        rows = lax.dot_general(table, twice[slot], NT, preferred_element_type=F32)
        wide[:, w, :128] = rows[:32]
        wide[:, w, 128:] = rows[32:]
    out_ref[...] = wide[...].astype(BF16)


def spectral_kernel(rows_ref, lon_ref, inverse_ref, small_ref, out_ref, modes):
    waves = jnp.dot(lon_ref[...], rows_ref[...], preferred_element_type=F32).astype(BF16)
    at_edge = lax.axis_index("zl") + lax.axis_index("y") + lax.axis_index("core") == 0
    row = lax.broadcasted_iota(jnp.int32, (256, 8), 0) // 64
    spot = lax.broadcasted_iota(jnp.int32, (256, 8), 1)
    blocks = jnp.where(row == spot, 1.0, 0.0).astype(BF16)
    down64 = lax.broadcasted_iota(jnp.int32, (256, 64), 0) % 64
    stack = jnp.where(down64 == lax.broadcasted_iota(jnp.int32, (256, 64), 1), 1.0, 0.0).astype(BF16)

    def tables(weights, signs, columns):
        lane = lax.broadcasted_iota(jnp.int32, (64, columns), 1) % 64
        spread = jnp.where(lane == lax.broadcasted_iota(jnp.int32, (64, columns), 0), 1.0, 0.0)
        spread = spread.astype(BF16)
        tiles = []
        for part in range(2):
            tall = jnp.dot(stack, weights[part], preferred_element_type=F32).astype(BF16)
            tiles.append(jnp.dot(tall, spread, preferred_element_type=F32))
        found = []
        for kind in (0, 2):
            mask = [
                jnp.dot(blocks, signs[kind + part], preferred_element_type=F32)
                for part in range(2)
            ]
            found.append(tiles[0] * mask[0] + tiles[1] * mask[1])
        plain, edge = found
        return [jnp.where(at_edge, edge, plain).astype(BF16), plain.astype(BF16)]

    def rows_of(start, count):
        return small_ref[start : start + count]

    first = [rows_of(160 + 64 * part, 64)[:, :64] for part in range(2)]
    second = [rows_of(288 + 64 * part, 64)[:, :64] for part in range(2)]
    signs_in = [rows_of(64 + 8 * kind, 8) for kind in range(4)]
    signs_out = [
        jnp.concatenate([rows_of(96 + 8 * kind, 8), rows_of(128 + 8 * kind, 8)], axis=1)
        for kind in range(4)
    ]
    mix_in = tables(first, signs_in, 256)
    mix_out = tables(second, signs_out, 512)
    for pair in range(2):
        lanes = slice(pair * 128, pair * 128 + 128)
        middle = jnp.dot(waves[:KW, lanes], mix_in[pair][:128], preferred_element_type=F32)
        middle += jnp.dot(waves[KW:, lanes], mix_in[pair][128:], preferred_element_type=F32)
        middle = jnp.maximum(middle, 0.0).astype(BF16)
        back = shrink(jnp.dot(middle, mix_out[pair], preferred_element_type=F32))
        modes[:KW, lanes] = (back[:, :128] + back[:, 128:256]).astype(BF16)
        modes[KW:, lanes] = (back[:, 256:384] + back[:, 384:]).astype(BF16)
    out_ref[...] = jnp.dot(inverse_ref[...], modes[...], preferred_element_type=F32).astype(BF16)


def inverse_kernel(rows_ref, tokens_ref, normed_ref, small_ref, mixed_ref, wide):
    wide[...] = rows_ref[...].astype(F32)
    table = small_ref[:64]
    for w in range(16):
        rows = jnp.concatenate([wide[:, w, :128], wide[:, w, 128:]]).astype(BF16)
        both = lax.dot_general(rows, table, TN, preferred_element_type=F32)
        filtered = (both[:64, :LAT] + both[64:, LAT:]).astype(BF16).astype(F32)
        mixed = tokens_ref[w].astype(F32) + normed_ref[w].astype(F32) + filtered
        mixed_ref[0, w // 2, w % 2] = mixed.astype(BF16)
        mixed_ref[1, w // 2, w % 2] = mixed.astype(BF16)


def second_norm_kernel(mixed_ref, sums_ref, out_ref):
    for w in range(2):
        wide = mixed_ref[:, w].astype(F32).reshape(C, 128)
        mean = jnp.sum(wide, axis=0, keepdims=True) / C
        power = jnp.sum(wide * wide, axis=0, keepdims=True) / C - mean * mean
        scale = lax.rsqrt(power + EPSILON)
        for block in range(16):
            rows = slice(block * 64, block * 64 + 64)
            gain = column_of(sums_ref[block, 32:33, :64])
            values = mixed_ref[block, w].astype(F32)
            out = (values - mean) * scale * gain
            out_ref[rows, w * 128 : w * 128 + 128] = out.astype(BF16)


def mlp_kernel(*refs):
    p0, z0, z1, z2, x0, x12, x3, own_ref, other_ref, own_out, other_out = refs
    pieces = [p0, z0, z1, z2, x0, x12.at[0], x12.at[1], x3]
    group = jnp.concatenate([own_ref[...], other_ref[...]], axis=1)
    total = None
    for first, second in zip(pieces[0::2], pieces[1::2]):
        up = jnp.concatenate([first[0], second[0]])
        down = jnp.concatenate([first[1], second[1]])
        upward = jnp.dot(up, group, preferred_element_type=F32)
        hidden = jax.nn.gelu(upward).astype(BF16)
        found = lax.dot_general(down, hidden, TN, preferred_element_type=F32)
        total = found if total is None else total + found
    own_out[...] = total[:, :256]
    other_out[...] = total[:, 256:].astype(BF16)


def bring_kernel(source_ref, out_ref, sem):
    copy = pltpu.make_async_copy(source_ref, out_ref, sem)
    copy.start()
    copy.wait()


def bring(values):
    return pl.pallas_call(
        bring_kernel,
        out_shape=shape(values.shape),
        in_specs=[pl.BlockSpec(memory_space=pl.ANY)],
        out_specs=VMEM,
        scratch_shapes=[pltpu.SemaphoreType.DMA],
        compiler_params=PARAMS,
        name="bring",
    )(values)


def core_sum_kernel(own_ref, other_ref, keep_ref, send_ref):
    xh = lax.axis_index("xh")
    mine = pl.ds(pl.multiple_of(xh * 512, 512), 512)
    theirs = pl.ds(pl.multiple_of((1 - xh) * 512, 512), 512)
    keep_ref[...] = own_ref[mine] + other_ref[mine].astype(F32)
    send_ref[...] = (own_ref[theirs] + other_ref[theirs].astype(F32)).astype(BF16)


def finish_kernel(wide_ref, keep_ref, other_ref, out_ref):
    xh = lax.axis_index("xh")
    for d in range(8):
        rows = slice(d * 64, d * 64 + 64)
        branch = keep_ref[rows] + other_ref[1 - xh, rows].astype(F32)
        for w in range(2):
            sums = wide_ref[xh * 8 + d, w].astype(F32) + branch[:, w * 128 : w * 128 + 128]
            out_ref[d, w] = sums.astype(BF16)


def call(kernel, shapes, scratch, name, args, limit=10 << 20):
    specs = [VMEM] * len(args)
    many = isinstance(shapes, list)
    return pl.pallas_call(
        kernel,
        out_shape=shapes,
        in_specs=specs,
        out_specs=[VMEM] * len(shapes) if many else VMEM,
        scratch_shapes=scratch,
        compiler_params=pltpu.CompilerParams(vmem_limit_bytes=limit),
        name=name,
    )(*args)


def shape(dims, kind=BF16):
    return jax.ShapeDtypeStruct(dims, kind)


def swap(values, axis):
    return lax.ppermute(values, axis, [(0, 1), (1, 0)])


def next_pair(values):
    pairs = []
    for zh in range(4):
        pairs.append((4 + zh, (zh + 1) % 4))
        pairs.append((zh, 4 + (zh - 1) % 4))
    return lax.ppermute(values, ("zl", "zh"), pairs)


def per_device(grid_state, first_gain, spectral_first, spectral_second, second_gain, up_weight, down_weight):
    tokens = grid_state.transpose(1, 2, 0)
    packed, sums = setup(up_weight, down_weight, tokens, second_gain)
    z0 = next_pair(packed)
    x0 = swap(packed, "xl")
    sums = lax.all_to_all(sums, CH_AXES, 0, 0)
    signs_out = sign_rows(SIGNS_OUT).reshape(32, 512)
    small = jnp.concatenate(
        [
            jnp.asarray(lat_pairs(), BF16),
            jnp.asarray(sign_rows(SIGNS_IN).reshape(32, 256), BF16),
            jnp.asarray(signs_out[:, :256], BF16),
            jnp.asarray(signs_out[:, 256:], BF16),
            jnp.pad(spectral_first.reshape(128, 64), ((0, 0), (0, 192))),
            jnp.pad(spectral_second.reshape(128, 64), ((0, 0), (0, 192))),
            jnp.pad(first_gain[None], ((0, 15), (0, 192))),
        ]
    )
    sums, small, z0, x0 = lax.optimization_barrier((sums, small, z0, x0))
    normed, rows = call(
        forward_kernel,
        [shape((16, 64, 128)), shape((32, 16, 256))],
        [pltpu.VMEM((2, 128, 256), BF16), pltpu.VMEM((32, 16, 256), F32)],
        "norm_latitude",
        (sums, tokens, small),
    )
    rows, z0 = lax.optimization_barrier((rows, z0))
    z1 = swap(z0, "zl")
    rows = lax.all_to_all(rows, LON_AXES, 0, 0)
    rows, z1 = lax.optimization_barrier((rows, z1))
    x12 = swap(jnp.stack([z0, z1]), "xl")
    back = call(
        spectral_kernel,
        shape((LON, 256)),
        [pltpu.VMEM((LON, 256), BF16)],
        "spectral",
        (
            rows.reshape(LON, 256),
            jnp.asarray(lon_table(), BF16),
            jnp.asarray(lon_inverse_table(), BF16),
            small,
        ),
    )
    back, z1 = lax.optimization_barrier((back.reshape(32, 16, 256), z1))
    z2 = next_pair(z1)
    back = lax.all_to_all(back, LON_AXES, 0, 0)
    back, z2, x12 = lax.optimization_barrier((back, z2, x12))
    mixed = call(
        inverse_kernel,
        shape((2, 8, 2, 64, 128)),
        [pltpu.VMEM((32, 16, 256), F32)],
        "latitude_back",
        (back, tokens, normed, small),
    )
    mixed, z2 = lax.optimization_barrier((mixed, z2))
    x3 = swap(z2, "xl")
    wide = lax.all_to_all(mixed.reshape(16, 2, 64, 128), CH_AXES, 0, 0)
    wide = lax.optimization_barrier(wide)
    own = call(second_norm_kernel, shape((C, 256)), [], "second_norm", (wide, sums))
    own, late = lax.optimization_barrier((own, z2))
    late = bring(late)
    own_out, other_out = call(
        mlp_kernel,
        [shape((C, 256), F32), shape((C, 256))],
        [],
        "channel_mlp",
        (packed, z0, z1, late, x0, x12, x3, own, swap(own, "core")),
        limit=30 << 20,
    )
    keep, send = call(
        core_sum_kernel,
        [shape((512, 256), F32), shape((512, 256))],
        [],
        "core_sum",
        (own_out, swap(other_out, "core")),
    )
    result = call(finish_kernel, shape((8, 2, 64, 128)), [], "finish", (wide, keep, lax.all_gather(send, "xh", axis=0)))
    result = lax.all_to_all(lax.optimization_barrier(result), ("xl", "zh"), 0, 0)
    return result.reshape(16, 64, 128).transpose(2, 0, 1)


def solution(mesh):
    fine = Mesh(
        mesh.devices.reshape(2, 8, 2, 2, 2, 4), ("zl", "y", "core", "xh", "xl", "zh")
    )
    return jax.shard_map(
        per_device,
        mesh=fine,
        in_specs=(
            P(None, LON_AXES, CH_AXES),
            P(CH_AXES),
            P(None, CH_AXES, None),
            P(None, CH_AXES, None),
            P(CH_AXES),
            P(None, CH_AXES),
            P(CH_AXES, None),
        ),
        out_specs=P(None, LON_AXES, CH_AXES),
        check_vma=False,
    )
```
